32 devices in a mesh: group: 4 (over y, x), blk: 8 (over z, core).
Axes of the slice: x: 2, y: 2, z: 4, core: 2. Of those that a mesh axis runs over, the one named last changes fastest.
Arguments:
- embeddings: float32 [18432, 1024], P(('group', 'blk')), may hold values from -100 to 100
- cluster: int32 [18432], P(('group', 'blk')), may hold values from 0 to 63, as said below
- global_index: int32 [18432], P(('group', 'blk')), may hold values from 0 to 18431, each once
- send_counts: int32 [32, 4], P(('group', 'blk')), may hold values from 1 to 216, as said below
Outputs:
- best_cosine: float32 [18432], P(('group', 'blk'))
The draws below stay inside these ranges and needn't reach their ends.
Inputs may be any that keep to these rules, and one draw needn't show every extreme that they name: The row's cluster group is given by send_counts; of the rows that one device sends to one cluster group, at most 27 have a cluster number in any one block c // 8 of consecutive cluster numbers, and every device has exactly 27 in some block. `global_index`: each number once over all devices. The 4 counts of a device sum to 576; its rows stand in order of cluster group, send_counts[d,g] of them for group g; every device has a count of exactly 216.
All inputs are finite; a program needn't handle non-finite values.
Results may differ from the reference program's by a relative error of at most 0.0003.
Values may be sent and summed in bfloat16 or wider, within the bound.
A program may use at most 128 MiB of HBM per device.

```python
import math
import jax
import jax.numpy as jnp
from jax import lax

E = 1024
ROWS_DEV = 576
KLOC = 64
CAP = 216
IPG = 4608
TOTAL = 18432
N_GROUP = 4
N_BLK = 8
DEVICES = 32


def layout(key):
    spread = ROWS_DEV - CAP
    share = spread // (N_GROUP - 1)
    leftover = spread - share * (N_GROUP - 1)
    jitter = max(0, min(share - 1, CAP - share - 1))
    busiest = jax.random.randint(jax.random.fold_in(key, 11), (DEVICES,), 0, N_GROUP)
    raised = jax.random.randint(jax.random.fold_in(key, 12), (DEVICES, N_GROUP - 1), 0, jitter + 1)
    others = share + raised - jnp.roll(raised, -1, axis=1) + (jnp.arange(N_GROUP - 1) < leftover).astype(jnp.int32)
    column = jnp.arange(N_GROUP, dtype=jnp.int32)
    later = (column[None, :] > busiest[:, None]).astype(jnp.int32)
    pick_index = jnp.clip(column[None, :] - later, 0, N_GROUP - 2)
    counts = jnp.where(column[None, :] == busiest[:, None], CAP, jnp.take_along_axis(others, pick_index, axis=1)).astype(jnp.int32)
    cum_ends = jnp.cumsum(counts, axis=1).astype(jnp.int32)
    starts = cum_ends - counts
    position = jnp.arange(ROWS_DEV, dtype=jnp.int32)
    owner_dev = jnp.sum((position[None, :, None] >= cum_ends[:, None, :]).astype(jnp.int32), axis=2)
    in_run = position[None, :] - jnp.take_along_axis(starts, owner_dev, axis=1)
    run_keys = jax.random.split(jax.random.fold_in(key, 14), DEVICES * N_GROUP)
    orders = jax.vmap(lambda one_key: jax.random.permutation(one_key, N_BLK))(run_keys).astype(jnp.int32)
    run_row = jnp.arange(DEVICES, dtype=jnp.int32)[:, None] * N_GROUP + owner_dev
    block_of = orders[run_row.reshape(-1), (in_run % N_BLK).reshape(-1)]
    per_block = KLOC // N_BLK
    inner = jax.random.randint(jax.random.fold_in(key, 13), (TOTAL,), 0, per_block)
    cluster_ids = (block_of * per_block + inner).astype(jnp.int32)
    repeat = jax.random.randint(jax.random.fold_in(key, 15), (TOTAL,), 0, IPG // KLOC)
    item_local = cluster_ids + KLOC * repeat
    owner_group = owner_dev.reshape(-1)
    item_global = owner_group * IPG + item_local
    return (counts, owner_group, item_global, cluster_ids)


def draw_send_counts(key, part):
    return layout(key)[0]


def draw_cluster(key, part):
    return layout(key)[3]


def draw_embeddings(key, part):
    counts, owner_group, item_global, cluster_ids = layout(key)
    centers = jax.random.normal(jax.random.fold_in(key, 21), (N_GROUP * KLOC, E), jnp.float32)
    center_rows = jnp.take(centers, owner_group * KLOC + cluster_ids, axis=0)
    shared_key = jax.random.fold_in(key, 22)

    def item_normal(item_id):
        return jax.random.normal(jax.random.fold_in(shared_key, item_id), (E,), jnp.float32)
    fresh_key = jax.random.fold_in(key, 23)
    mix_weight = jnp.exp(jax.random.uniform(jax.random.fold_in(key, 24), (TOTAL, 1), jnp.float32, math.log(0.2), math.log(2.0)))
    shared = jax.vmap(item_normal)(item_global)
    fresh = jax.random.normal(fresh_key, (TOTAL, E), jnp.float32)
    row_scale = jnp.exp(jax.random.uniform(jax.random.fold_in(key, 25), (TOTAL, 1), jnp.float32, math.log(0.5), math.log(5.0)))
    values = row_scale * (mix_weight * center_rows + shared + 0.5 * fresh)
    return jnp.clip(values, -100.0, 100.0).astype(jnp.float32)


def setup_inputs(seed: int = 0) -> dict:
    arg_keys = jax.random.split(jax.random.key(seed), 5)
    embeddings = draw_embeddings(jax.random.fold_in(arg_keys[4], 71), 0)
    cluster = draw_cluster(jax.random.fold_in(arg_keys[4], 71), 0)
    global_index = jax.random.permutation(arg_keys[2], TOTAL).astype(jnp.int32)
    send_counts = draw_send_counts(jax.random.fold_in(arg_keys[4], 71), 0)
    return {"embeddings": embeddings, "cluster": cluster, "global_index": global_index, "send_counts": send_counts}


def reference(embeddings, cluster, global_index, send_counts):
    squares = lax.optimization_barrier(jnp.sum(embeddings * embeddings, axis=1, keepdims=True))
    unit_rows = (embeddings * lax.rsqrt(squares + 1e-06)).astype(jnp.bfloat16)
    cum_ends = jnp.cumsum(send_counts, axis=1).astype(jnp.int32)
    position = jnp.arange(ROWS_DEV, dtype=jnp.int32)
    owner_group = lax.optimization_barrier(jnp.sum((position[None, :, None] >= cum_ends[:, None, :]).astype(jnp.int32), axis=2)).reshape(-1)
    sort_key = (owner_group * KLOC + cluster).astype(jnp.int32)
    sort_order = jnp.argsort(sort_key, stable=True).astype(jnp.int32)
    block_rows = 512
    block_count = -(-TOTAL // block_rows)
    extra_rows = block_count * block_rows - TOTAL
    sorted_key = jnp.concatenate([sort_key[sort_order], jnp.full((extra_rows,), N_GROUP * KLOC, jnp.int32)])
    sorted_ids = jnp.concatenate([global_index[sort_order], jnp.zeros((extra_rows,), jnp.int32)])
    sorted_rows = jnp.concatenate([unit_rows[sort_order].astype(jnp.float32), jnp.zeros((extra_rows, E), jnp.float32)])

    def one_block(block_index):
        first_row = (block_index * block_rows).astype(jnp.int32)
        q_rows = lax.dynamic_slice_in_dim(sorted_rows, first_row, block_rows, 0)
        q_key = lax.dynamic_slice_in_dim(sorted_key, first_row, block_rows, 0)
        q_ids = lax.dynamic_slice_in_dim(sorted_ids, first_row, block_rows, 0)
        low_edge = jnp.searchsorted(sorted_key, q_key[0], side='left').astype(jnp.int32)
        high_edge = jnp.searchsorted(sorted_key, q_key[block_rows - 1], side='right').astype(jnp.int32)

        def scan_keys(key_block, best_now):
            key_start = (key_block * block_rows).astype(jnp.int32)
            key_rows = lax.dynamic_slice_in_dim(sorted_rows, key_start, block_rows, 0)
            key_label = lax.dynamic_slice_in_dim(sorted_key, key_start, block_rows, 0)
            key_ids = lax.dynamic_slice_in_dim(sorted_ids, key_start, block_rows, 0)
            cosine = jnp.dot(q_rows, key_rows.T, preferred_element_type=jnp.float32, precision=lax.Precision.HIGHEST)
            usable = (q_key[:, None] == key_label[None, :]) & (key_ids[None, :] < q_ids[:, None])
            return jnp.maximum(best_now, lax.optimization_barrier(jnp.max(jnp.where(usable, cosine, jnp.float32(-1.0)), axis=1)))
        start_block = (low_edge // block_rows).astype(jnp.int32)
        stop_block = ((high_edge - 1) // block_rows + 1).astype(jnp.int32)
        return lax.fori_loop(start_block, stop_block, scan_keys, jnp.full((block_rows,), -1.0, jnp.float32))
    results = lax.map(one_block, jnp.arange(block_count, dtype=jnp.int32)).reshape(-1)[:TOTAL]
    return jnp.zeros((TOTAL,), jnp.float32).at[sort_order].set(results)
```

```python
import functools

import jax
import jax.numpy as jnp
from jax import lax
from jax.experimental import pallas as pl
from jax.experimental.pallas import tpu as pltpu
from jax.sharding import PartitionSpec as P

CLUSTERS = 64
MESH = pl.DeviceIdType.MESH
NT = (((1,), (1,)), ((), ()))
TN = (((0,), (0,)), ((), ()))


def iota(shape, dim):
    return lax.broadcasted_iota(jnp.int32, shape, dim)


def kernel(groups, blocks, pad, folds, high, cnt_ref, cl_ref, gid_ref, emb_ref, out_ref,
           packed, recv, unit, back, home, send_sem, recv_sem, bsend_sem, brecv_sem, self_sem):
    rows, width = emb_ref.shape
    n = groups * blocks
    slots = n * pad
    per_block = CLUSTERS // blocks
    me = lax.axis_index("group") * blocks + lax.axis_index("blk")

    def at(dev):
        return {"group": dev // blocks, "blk": lax.rem(dev, blocks)}

    def ahead(i):
        return lax.rem(me + i, n)

    def behind(i):
        return lax.rem(me + n - i, n)

    barrier = pltpu.get_barrier_semaphore()

    def greet(i, c):
        pl.semaphore_signal(barrier, inc=1, device_id=at(ahead(i)), device_id_type=MESH)
        return c

    lax.fori_loop(1, n, greet, 0)

    pos = iota((1, rows), 1)
    owner = jnp.zeros((1, rows), jnp.int32)
    end = jnp.int32(0)
    for g in range(groups):
        end = end + cnt_ref[0, g]
        owner += (pos >= end).astype(jnp.int32)
    owner = jnp.minimum(owner, groups - 1)
    cl = cl_ref[...]
    gid = gid_ref[...]
    dest = owner * blocks + cl // per_block
    rel = jnp.where(dest >= me, dest - me, dest - me + n)
    hot = iota((n, rows), 0) == rel
    hot_f = hot.astype(jnp.float32)
    upper = (iota((rows, rows), 0) < iota((rows, rows), 1)).astype(jnp.float32).astype(jnp.bfloat16)
    before = jnp.dot(hot_f.astype(jnp.bfloat16), upper, preferred_element_type=jnp.float32)
    rank = jnp.sum(hot_f * before, axis=0, keepdims=True).astype(jnp.int32)
    slot = rel * pad + rank

    digits = (
        (cl % per_block + 1) * high + gid // 65536,
        (gid // 256) % 256,
        gid % 256,
    )
    amounts = jnp.concatenate([hot_f * d.astype(jnp.float32) for d in digits], axis=0)
    lane0 = lax.rem(me * pad, width)
    half = (me * pad) // width
    spots = (iota((width, rows), 0) == rank + lane0).astype(jnp.float32).astype(jnp.bfloat16)
    meta = lax.dot_general(
        amounts.astype(jnp.bfloat16), spots, NT, preferred_element_type=jnp.float32
    ).astype(jnp.bfloat16)
    m = iota((1, 3 * n), 1)
    place = (m % n) * pad + (pad - 3 * folds) + (m // n) * folds + half

    x = emb_ref[...]
    squares = jnp.sum(x * x, axis=1, keepdims=True)
    unit[...] = (x * lax.rsqrt(squares + 1e-06)).astype(jnp.bfloat16)

    tile = 256
    per_tile = tile // pad

    def out_copy(i):
        return pltpu.make_async_remote_copy(
            src_ref=packed.at[pl.ds(pl.multiple_of(i * pad, pad), pad)],
            dst_ref=recv.at[pl.ds(pl.multiple_of(me * pad, pad), pad)],
            send_sem=send_sem.at[i], recv_sem=recv_sem.at[i],
            device_id=at(ahead(i)), device_id_type=MESH,
        )

    def own_copy():
        return pltpu.make_async_copy(
            packed.at[pl.ds(0, pad)], recv.at[pl.ds(pl.multiple_of(me * pad, pad), pad)], self_sem)

    def send(i, c):
        out_copy(i).start()
        return c

    for t in range(slots // tile):
        pick = (iota((tile, rows), 0) + t * tile == slot).astype(jnp.float32).astype(jnp.bfloat16)
        pick_m = (iota((tile, 3 * n), 0) + t * tile == place).astype(jnp.float32).astype(jnp.bfloat16)
        block = jnp.dot(pick, unit[...], preferred_element_type=jnp.float32)
        block += jnp.dot(pick_m, meta, preferred_element_type=jnp.float32)
        packed[t * tile:(t + 1) * tile, :] = block.astype(jnp.bfloat16)
        if t == 0:
            pl.semaphore_wait(barrier, n - 1)
            own_copy().start()
        lax.fori_loop(max(1, t * per_tile), (t + 1) * per_tile, send, 0)

    own_copy().wait()

    def arrive(i, c):
        out_copy(i).wait_recv()
        return c

    lax.fori_loop(1, n, arrive, 0)

    total = jnp.zeros((16, width), jnp.float32)
    for b in range(n):
        total += recv[b * pad + pad - 16:b * pad + pad, :].astype(jnp.float32)
    base = 16 - 3 * folds
    parts = [
        jnp.concatenate([total[base + k * folds + h:base + k * folds + h + 1, :] for h in range(folds)], axis=1)
        [:, :slots] for k in range(3)
    ]
    key_row = parts[0] * 65536.0 + parts[1] * 256.0 + parts[2]
    low_row = jnp.floor(parts[0] * (1.0 / high)) * (high * 65536.0)
    key_col = jnp.transpose(jnp.broadcast_to(key_row, (8, slots)))[:, 0:1]

    for t in range(slots // tile):
        lanes = slice(t * tile, (t + 1) * tile)
        cosine = lax.dot_general(recv[...], recv[lanes, :], NT, preferred_element_type=jnp.float32)
        usable = (key_col >= low_row[:, lanes]) & (key_col < key_row[:, lanes])
        best = jnp.max(jnp.where(usable, cosine, jnp.float32(-1.0)), axis=0, keepdims=True)
        for u in range(tile // 128):
            c = t * (tile // 128) + u
            back[c * 8:(c + 1) * 8, :] = jnp.broadcast_to(best[:, u * 128:(u + 1) * 128], (8, 128))

    def back_copy(i):
        to = behind(i)
        chunk = (to * pad) // 128
        return pltpu.make_async_remote_copy(
            src_ref=back.at[pl.ds(pl.multiple_of(chunk * 8, 8), 8)],
            dst_ref=home.at[pl.ds(pl.multiple_of(i * 8, 8), 8)],
            send_sem=bsend_sem.at[i], recv_sem=brecv_sem.at[i],
            device_id=at(to), device_id_type=MESH,
        )

    def give(i, c):
        back_copy(i).start()
        return c

    lax.fori_loop(1, n, give, 0)
    mine = pltpu.make_async_copy(
        back.at[pl.ds(pl.multiple_of(((me * pad) // 128) * 8, 8), 8)], home.at[pl.ds(0, 8)], self_sem)
    mine.start()
    mine.wait()

    def take(i, c):
        back_copy(i).wait_recv()
        return c

    lax.fori_loop(1, n, take, 0)

    hot8 = (iota((n * 8, rows), 0) == rel * 8).astype(jnp.float32)
    found = lax.dot_general(home[...], hot8, TN, precision=lax.Precision.HIGHEST,
                            preferred_element_type=jnp.float32)
    off = lax.rem(me * pad, 128)
    out_ref[...] = jnp.sum(
        jnp.where(iota((128, rows), 0) == rank + off, found, 0.0), axis=0, keepdims=True)

    def done(i, c):
        out_copy(i).wait_send()
        back_copy(i).wait_send()
        return c

    lax.fori_loop(1, n, done, 0)


def on_device(embeddings, cluster, global_index, send_counts):
    rows, width = embeddings.shape
    groups = lax.axis_size("group")
    blocks = lax.axis_size("blk")
    n = groups * blocks
    capacity = -(-(3 * rows // (2 * groups)) // blocks)
    pad = 16
    while True:
        folds = -(-n * pad // width)
        if capacity + 3 * folds <= pad:
            break
        pad += 16
    high = (n * rows - 1) // 65536 + 1
    slots = n * pad
    best = pl.pallas_call(
        functools.partial(kernel, groups, blocks, pad, folds, high),
        out_shape=jax.ShapeDtypeStruct((1, rows), jnp.float32),
        in_specs=[pl.BlockSpec(memory_space=pltpu.SMEM)] + [pl.BlockSpec(memory_space=pltpu.VMEM)] * 3,
        out_specs=pl.BlockSpec(memory_space=pltpu.VMEM),
        scratch_shapes=[
            pltpu.VMEM((slots, width), jnp.bfloat16),
            pltpu.VMEM((slots, width), jnp.bfloat16),
            pltpu.VMEM((rows, width), jnp.bfloat16),
            pltpu.VMEM((slots // 128 * 8, 128), jnp.float32),
            pltpu.VMEM((n * 8, 128), jnp.float32),
            pltpu.SemaphoreType.DMA((n,)),
            pltpu.SemaphoreType.DMA((n,)),
            pltpu.SemaphoreType.DMA((n,)),
            pltpu.SemaphoreType.DMA((n,)),
            pltpu.SemaphoreType.DMA,
        ],
        compiler_params=pltpu.CompilerParams(
            collective_id=0, has_side_effects=True, vmem_limit_bytes=48 * 1024 * 1024
        ),
    )(send_counts, cluster.reshape(1, rows), global_index.reshape(1, rows), embeddings)
    return best.reshape(rows)


def solution(mesh):
    placed = (
        P(("group", "blk"), None),
        P(("group", "blk")),
        P(("group", "blk")),
        P(("group", "blk"), None),
    )
    return jax.shard_map(
        on_device, mesh=mesh, in_specs=placed, out_specs=P(("group", "blk")), check_vma=False
    )
```

```python
import functools

import jax
import jax.numpy as jnp
from jax import lax
from jax.experimental import pallas as pl
from jax.experimental.pallas import tpu as pltpu
from jax.sharding import PartitionSpec as P

CLUSTERS = 64
SUB = 16
SPAN = 32
TILE = 256
MESH = pl.DeviceIdType.MESH
NT = (((1,), (1,)), ((), ()))
TN = (((0,), (0,)), ((), ()))
F32 = jnp.float32
BF16 = jnp.bfloat16


def iota(shape, dim):
    return lax.broadcasted_iota(jnp.int32, shape, dim)


def hot_of(mask):
    return mask.astype(F32).astype(BF16)


def kernel(groups, blocks, full, tail, keep, high, cnt_hbm, cl_hbm, gid_hbm, emb_hbm, out_ref,
           cnt_ref, cl_ref, gid_ref, emb_ref, packed, recv, unit, late, back, home,
           in_sem, send_sem, recv_sem, bsend_sem, brecv_sem, self_sem):
    rows, width = emb_ref.shape
    n = groups * blocks
    band = n * SUB
    parts = full + 1
    per_block = CLUSTERS // blocks
    lows = blocks // 2
    rest = width - keep
    per = keep // rest if rest else 1
    shift = full * width
    my_g = lax.axis_index("group")
    my_b = lax.axis_index("blk")
    my_hi, my_lo = my_b // lows, lax.rem(my_b, lows)
    me = my_g * blocks + my_b

    def peer(i, way):
        hi = lax.rem(my_hi + 1 - i // (n // 2), 2)
        j = lax.rem(i, n // 2)
        dl, dg = j // groups, lax.rem(j, groups)
        if way < 0:
            dl, dg = lows - dl, groups - dg
        lo = lax.rem(my_lo + dl, lows)
        g = lax.rem(my_g + dg, groups)
        return g, hi * lows + lo

    def others(act, lo=0, hi=None):
        hi = n if hi is None else hi

        def body(i, c):
            act(i)
            return c

        if lo < n // 2:
            lax.fori_loop(lo, min(hi, n // 2), body, 0)
        if hi > n // 2 + 1:
            lax.fori_loop(max(lo, n // 2 + 1), hi, body, 0)

    loads = [
        pltpu.make_async_copy(a, b, in_sem.at[k])
        for k, (a, b) in enumerate(
            ((cnt_hbm, cnt_ref), (cl_hbm, cl_ref), (gid_hbm, gid_ref), (emb_hbm, emb_ref)))
    ]
    for load in loads:
        load.start()

    barrier = pltpu.get_barrier_semaphore()

    def greet(i):
        g, b = peer(i, 1)
        pl.semaphore_signal(barrier, inc=1, device_id={"group": g, "blk": b}, device_id_type=MESH)

    others(greet)

    for load in loads[:3]:
        load.wait()
    pos = iota((1, rows), 1)
    owner = jnp.zeros((1, rows), jnp.int32)
    end = jnp.zeros((1, 1), jnp.int32)
    for g in range(groups - 1):
        end = end + cnt_ref[0:1, g:g + 1]
        owner += (pos >= end).astype(jnp.int32)
    cl = cl_ref[...].reshape(1, rows)
    gid = gid_ref[...].reshape(1, rows)
    to_b = cl // per_block
    to_hi, to_lo = to_b // lows, to_b % lows
    step = (
        jnp.where(to_hi == my_hi, n // 2, 0)
        + ((to_lo + lows - my_lo) % lows) * groups
        + (owner + groups - my_g) % groups
    )
    hot = (iota((n, rows), 0) == step).astype(F32)
    hot_b = hot.astype(BF16)
    upper = hot_of(iota((rows, rows), 0) < iota((rows, rows), 1))
    before = jnp.dot(hot_b, upper, preferred_element_type=F32)
    rank = jnp.sum(hot * before, axis=0, keepdims=True).astype(jnp.int32)
    u = rank - full * SUB
    first = step * SUB

    digits = (
        (cl % per_block + 1) * high + gid // 65536,
        (gid // 256) % 256,
        gid % 256,
    )
    lane = iota((128, rows), 0)
    spots = jnp.zeros((128, rows), F32)
    for k, d in enumerate(digits):
        spots = jnp.where(lane == rank + k * SPAN, d.astype(F32), spots)
    meta = lax.dot_general(hot_b, spots.astype(BF16), NT, preferred_element_type=F32).astype(BF16)

    slots = [jnp.where(rank // SUB == p, first + rank % SUB, -1) for p in range(full)]
    slots.append(jnp.where(u >= 0, first + u, -1))
    if rest:
        slots += [jnp.where((u >= 0) & (u % per == j), first + tail + u // per, -1) for j in range(per)]

    loads[3].wait()
    x = emb_ref[...]
    squares = jnp.sum(x * x, axis=1, keepdims=True)
    unit[...] = (x * lax.rsqrt(squares + 1e-06)).astype(BF16)

    mine = pl.ds(pl.multiple_of(me * SUB, SUB), SUB)

    def out_copy(i):
        g, b = peer(i, 1)
        return pltpu.make_async_remote_copy(
            src_ref=packed.at[pl.ds(pl.multiple_of(i * SUB, SUB), SUB)],
            dst_ref=recv.at[mine],
            send_sem=send_sem, recv_sem=recv_sem,
            device_id={"group": g, "blk": b}, device_id_type=MESH,
        )

    for t in range(band // TILE):
        rows_t = slice(t * TILE, (t + 1) * TILE)
        at_row = iota((TILE, rows), 0) + t * TILE
        for p in range(full):
            packed[rows_t, p * width:(p + 1) * width] = jnp.dot(
                hot_of(at_row == slots[p]), unit[...], preferred_element_type=F32).astype(BF16)
        last = jnp.dot(hot_of(at_row == slots[full]), unit[:, :keep], preferred_element_type=F32)
        if rest:
            extra = [
                jnp.dot(hot_of(at_row == slots[full + 1 + j]), unit[:, keep:], preferred_element_type=F32)
                for j in range(per)
            ]
            last += jnp.concatenate(extra, axis=1)
        where = hot_of(iota((TILE, n), 0) + t * TILE == iota((TILE, n), 1) * SUB + SUB - 1)
        info = jnp.dot(where, meta, preferred_element_type=F32)
        packed[rows_t, shift:shift + 128] = (last[:, :128] + info).astype(BF16)
        packed[rows_t, shift + 128:shift + keep] = last[:, 128:].astype(BF16)
        if t == 0:
            pl.semaphore_wait(barrier, n - 1)
        others(lambda i: out_copy(i).start(), t * TILE // SUB, (t + 1) * TILE // SUB)

    own = pltpu.make_async_copy(packed.at[pl.ds(band // 2, SUB)], recv.at[mine], self_sem)
    own.start()
    own.wait()

    def all_rows():
        g, b = peer(0, 1)
        most = pl.ds(0, (n - 1) * SUB)
        return pltpu.make_async_remote_copy(
            src_ref=packed.at[most], dst_ref=recv.at[most], send_sem=send_sem, recv_sem=recv_sem,
            device_id={"group": g, "blk": b}, device_id_type=MESH)

    all_rows().wait_recv()

    total = parts * band
    take = hot_of(iota((n, band), 1) == iota((n, band), 0) * SUB + SUB - 1)
    info = jnp.dot(take, recv[:, shift:shift + 128], preferred_element_type=F32)
    which = iota((n, 128), 1) // SPAN
    info = jnp.concatenate([jnp.where(which == k, info, 0.0) for k in range(3)], axis=0).astype(BF16)
    at = iota((128, total), 1)
    spread = hot_of(iota((128, total), 0) % SPAN == at // band * SUB + at % SUB)
    wide = jnp.dot(info, spread, preferred_element_type=F32)
    source = (iota((n, total), 1) % band) // SUB == iota((n, total), 0)
    d0, d1, d2 = (
        jnp.sum(jnp.where(source, wide[k * n:(k + 1) * n], 0.0), axis=0, keepdims=True) for k in range(3)
    )
    key_row = d0 * 65536.0 + d1 * 256.0 + d2
    low_row = jnp.floor(d0 * (1.0 / high)) * (high * 65536.0)
    key_col = jnp.transpose(jnp.broadcast_to(key_row, (8, total)))[:, 0:1]

    late[:, :keep] = recv[:, shift:shift + keep]
    if rest:
        a, b = iota((TILE, TILE), 0), iota((TILE, TILE), 1)
        v = a % SUB
        for t in range(band // TILE):
            rows_t = slice(t * TILE, (t + 1) * TILE)
            found = jnp.zeros((TILE, rest), F32)
            for j in range(per):
                pick = (a // SUB == b // SUB) & (v < tail) & (v % per == j) & (b % SUB == tail + v // per)
                found += jnp.dot(
                    hot_of(pick), recv[rows_t, shift + j * rest:shift + (j + 1) * rest],
                    preferred_element_type=F32)
            late[rows_t, keep:] = found.astype(BF16)

    def part(p, lo, hi):
        return recv[lo:hi, p * width:(p + 1) * width] if p < full else late[lo:hi, :]

    for t in range(total // TILE):
        lanes = slice(t * TILE, (t + 1) * TILE)
        p, lo = t * TILE // band, t * TILE % band
        query = part(p, lo, lo + TILE)
        best = jnp.full((1, TILE), -1.0, F32)
        for q in range(parts):
            cosine = lax.dot_general(part(q, 0, band), query, NT, preferred_element_type=F32)
            keys = key_col[q * band:(q + 1) * band]
            usable = (keys >= low_row[:, lanes]) & (keys < key_row[:, lanes])
            best = jnp.maximum(best, jnp.max(jnp.where(usable, cosine, -1.0), axis=0, keepdims=True))
        for w in range(TILE // 128):
            back[lo // 128 + w, p:p + 1, :] = best[:, w * 128:(w + 1) * 128]

    def back_copy(i):
        g, b = peer(i, -1)
        return pltpu.make_async_remote_copy(
            src_ref=back.at[((g * blocks + b) * SUB) // 128], dst_ref=home.at[i],
            send_sem=bsend_sem, recv_sem=brecv_sem,
            device_id={"group": g, "blk": b}, device_id_type=MESH,
        )

    others(lambda i: back_copy(i).start())
    own_back = pltpu.make_async_copy(back.at[(me * SUB) // 128], home.at[n // 2], self_sem)
    own_back.start()
    own_back.wait()

    def all_back():
        g, b = peer(0, -1)
        most = home.at[pl.ds(0, n - 1)]
        return pltpu.make_async_remote_copy(
            src_ref=most, dst_ref=most, send_sem=bsend_sem, recv_sem=brecv_sem,
            device_id={"group": g, "blk": b}, device_id_type=MESH)

    all_back().wait_recv()

    found = jnp.zeros((128, rows), F32)
    for p in range(parts):
        found += lax.dot_general(
            home[:, p, :], jnp.where(rank // SUB == p, hot, 0.0), TN,
            precision=lax.Precision.HIGHEST, preferred_element_type=F32)
    off = lax.rem(me * SUB, 128)
    result = jnp.sum(jnp.where(lane == rank % SUB + off, found, 0.0), axis=0, keepdims=True)
    out_ref[...] = result.reshape(rows)
    all_rows().wait_send()
    all_back().wait_send()


def on_device(embeddings, cluster, global_index, send_counts):
    rows, width = embeddings.shape
    groups = lax.axis_size("group")
    blocks = lax.axis_size("blk")
    n = groups * blocks
    capacity = -(-(3 * rows // (2 * groups)) // blocks)
    full, tail = capacity // SUB, capacity % SUB
    for keep in (width // 2, 3 * width // 4, width):
        rest = width - keep
        if tail + (-(-tail // (keep // rest)) if rest else 0) < SUB:
            break
    high = (n * rows - 1) // 65536 + 1
    band = n * SUB
    lanes = full * width + keep
    anywhere = pl.BlockSpec(memory_space=pltpu.HBM)
    return pl.pallas_call(
        functools.partial(kernel, groups, blocks, full, tail, keep, high),
        out_shape=jax.ShapeDtypeStruct((rows,), F32),
        in_specs=[anywhere] * 4,
        out_specs=pl.BlockSpec(memory_space=pltpu.VMEM),
        scratch_shapes=[
            pltpu.VMEM((1, groups), jnp.int32),
            pltpu.VMEM((rows,), jnp.int32),
            pltpu.VMEM((rows,), jnp.int32),
            pltpu.VMEM((rows, width), F32),
            pltpu.VMEM((band, lanes), BF16),
            pltpu.VMEM((band, lanes), BF16),
            pltpu.VMEM((rows, width), BF16),
            pltpu.VMEM((band, width), BF16),
            pltpu.VMEM((band // 128, full + 1, 128), F32),
            pltpu.VMEM((n, full + 1, 128), F32),
            pltpu.SemaphoreType.DMA((4,)),
            pltpu.SemaphoreType.DMA,
            pltpu.SemaphoreType.DMA,
            pltpu.SemaphoreType.DMA,
            pltpu.SemaphoreType.DMA,
            pltpu.SemaphoreType.DMA,
        ],
        compiler_params=pltpu.CompilerParams(
            collective_id=0, has_side_effects=True, vmem_limit_bytes=48 * 1024 * 1024
        ),
    )(send_counts, cluster, global_index, embeddings)


def solution(mesh):
    placed = (
        P(("group", "blk"), None),
        P(("group", "blk")),
        P(("group", "blk")),
        P(("group", "blk"), None),
    )
    return jax.shard_map(
        on_device, mesh=mesh, in_specs=placed, out_specs=P(("group", "blk")), check_vma=False
    )
```

```python
import functools

import jax
import jax.numpy as jnp
from jax import lax
from jax.experimental import pallas as pl
from jax.experimental.pallas import tpu as pltpu
from jax.sharding import PartitionSpec as P

CLUSTERS = 64
SUB = 16
SPAN = 32
TILE = 256
MESH = pl.DeviceIdType.MESH
NT = (((1,), (1,)), ((), ()))
TN = (((0,), (0,)), ((), ()))
F32 = jnp.float32
BF16 = jnp.bfloat16


def iota(shape, dim):
    return lax.broadcasted_iota(jnp.int32, shape, dim)


def hot_of(mask):
    return mask.astype(F32).astype(BF16)


def kernel(groups, blocks, full, tail, keep, high, cnt_hbm, cl_hbm, gid_hbm, emb_hbm, out_ref,
           cnt_ref, cl_ref, gid_ref, emb_ref, packed, recv, unit, late, back, home,
           in_sem, send_sem, recv_sem, bsend_sem, brecv_sem, self_sem):
    rows, width = emb_ref.shape
    n = groups * blocks
    band = n * SUB
    parts = full + 1
    per_block = CLUSTERS // blocks
    lows = blocks // 2
    rest = width - keep
    per = keep // rest if rest else 1
    shift = full * width
    my_g = lax.axis_index("group")
    my_b = lax.axis_index("blk")
    my_hi, my_lo = my_b // lows, lax.rem(my_b, lows)
    me = my_g * blocks + my_b

    def peer(i, way):
        hi = lax.rem(my_hi + 1 - i // (n // 2), 2)
        j = lax.rem(i, n // 2)
        dl, dg = j // groups, lax.rem(j, groups)
        if way < 0:
            dl, dg = lows - dl, groups - dg
        lo = lax.rem(my_lo + dl, lows)
        g = lax.rem(my_g + dg, groups)
        return g, hi * lows + lo

    def others(act, lo=0, hi=None):
        hi = n if hi is None else hi

        def body(i, c):
            act(i)
            return c

        if lo < n // 2:
            lax.fori_loop(lo, min(hi, n // 2), body, 0)
        if hi > n // 2 + 1:
            lax.fori_loop(max(lo, n // 2 + 1), hi, body, 0)

    loads = [
        pltpu.make_async_copy(a, b, in_sem.at[k])
        for k, (a, b) in enumerate(
            ((cnt_hbm, cnt_ref), (cl_hbm, cl_ref), (gid_hbm, gid_ref), (emb_hbm, emb_ref)))
    ]
    for load in loads:
        load.start()

    barrier = pltpu.get_barrier_semaphore()

    def greet(i):
        g, b = peer(i, 1)
        pl.semaphore_signal(barrier, inc=1, device_id={"group": g, "blk": b}, device_id_type=MESH)

    others(greet)

    for load in loads[:3]:
        load.wait()
    pos = iota((1, rows), 1)
    owner = jnp.zeros((1, rows), jnp.int32)
    end = jnp.zeros((1, 1), jnp.int32)
    for g in range(groups - 1):
        end = end + cnt_ref[0:1, g:g + 1]
        owner += (pos >= end).astype(jnp.int32)
    cl = cl_ref[...].reshape(1, rows)
    gid = gid_ref[...].reshape(1, rows)
    to_b = cl // per_block
    to_hi, to_lo = to_b // lows, to_b % lows
    step = (
        jnp.where(to_hi == my_hi, n // 2, 0)
        + ((to_lo + lows - my_lo) % lows) * groups
        + (owner + groups - my_g) % groups
    )
    hot = (iota((n, rows), 0) == step).astype(F32)
    hot_b = hot.astype(BF16)
    upper = hot_of(iota((rows, rows), 0) < iota((rows, rows), 1))
    before = jnp.dot(hot_b, upper, preferred_element_type=F32)
    rank = jnp.sum(hot * before, axis=0, keepdims=True).astype(jnp.int32)
    u = rank - full * SUB
    first = step * SUB

    digits = (
        (cl % per_block + 1) * high + gid // 65536,
        (gid // 256) % 256,
        gid % 256,
    )
    lane = iota((128, rows), 0)
    spots = jnp.zeros((128, rows), F32)
    for k, d in enumerate(digits):
        spots = jnp.where(lane == rank + k * SPAN, d.astype(F32), spots)
    meta = lax.dot_general(hot_b, spots.astype(BF16), NT, preferred_element_type=F32).astype(BF16)

    slots = [jnp.where(rank // SUB == p, first + rank % SUB, -1) for p in range(full)]
    slots.append(jnp.where(u >= 0, first + u, -1))
    if rest:
        slots += [jnp.where((u >= 0) & (u % per == j), first + tail + u // per, -1) for j in range(per)]

    loads[3].wait()
    x = emb_ref[...]
    squares = jnp.sum(x * x, axis=1, keepdims=True)
    unit[...] = (x * lax.rsqrt(squares + 1e-06)).astype(BF16)

    mine = pl.ds(pl.multiple_of(me * SUB, SUB), SUB)

    def out_copy(i):
        g, b = peer(i, 1)
        return pltpu.make_async_remote_copy(
            src_ref=packed.at[pl.ds(pl.multiple_of(i * SUB, SUB), SUB)],
            dst_ref=recv.at[mine],
            send_sem=send_sem, recv_sem=recv_sem,
            device_id={"group": g, "blk": b}, device_id_type=MESH,
        )

    for t in range(band // TILE):
        rows_t = slice(t * TILE, (t + 1) * TILE)
        at_row = iota((TILE, rows), 0) + t * TILE
        for p in range(full):
            packed[rows_t, p * width:(p + 1) * width] = jnp.dot(
                hot_of(at_row == slots[p]), unit[...], preferred_element_type=F32).astype(BF16)
        last = jnp.dot(hot_of(at_row == slots[full]), unit[:, :keep], preferred_element_type=F32)
        if rest:
            extra = [
                jnp.dot(hot_of(at_row == slots[full + 1 + j]), unit[:, keep:], preferred_element_type=F32)
                for j in range(per)
            ]
            last += jnp.concatenate(extra, axis=1)
        where = hot_of(iota((TILE, n), 0) + t * TILE == iota((TILE, n), 1) * SUB + SUB - 1)
        info = jnp.dot(where, meta, preferred_element_type=F32)
        packed[rows_t, shift:shift + 128] = (last[:, :128] + info).astype(BF16)
        packed[rows_t, shift + 128:shift + keep] = last[:, 128:].astype(BF16)
        if t == 0:
            pl.semaphore_wait(barrier, n - 1)
        others(lambda i: out_copy(i).start(), t * TILE // SUB, (t + 1) * TILE // SUB)

    own = pltpu.make_async_copy(packed.at[pl.ds(band // 2, SUB)], recv.at[mine], self_sem)
    own.start()
    own.wait()

    def all_rows():
        g, b = peer(0, 1)
        most = pl.ds(0, (n - 1) * SUB)
        return pltpu.make_async_remote_copy(
            src_ref=packed.at[most], dst_ref=recv.at[most], send_sem=send_sem, recv_sem=recv_sem,
            device_id={"group": g, "blk": b}, device_id_type=MESH)

    all_rows().wait_recv()

    total = parts * band
    take = hot_of(iota((n, band), 1) == iota((n, band), 0) * SUB + SUB - 1)
    info = jnp.dot(take, recv[:, shift:shift + 128], preferred_element_type=F32)
    which = iota((n, 128), 1) // SPAN
    info = jnp.concatenate([jnp.where(which == k, info, 0.0) for k in range(3)], axis=0).astype(BF16)
    at = iota((128, total), 1)
    spread = hot_of(iota((128, total), 0) % SPAN == at // band * SUB + at % SUB)
    wide = jnp.dot(info, spread, preferred_element_type=F32)
    source = (iota((n, total), 1) % band) // SUB == iota((n, total), 0)
    d0, d1, d2 = (
        jnp.sum(jnp.where(source, wide[k * n:(k + 1) * n], 0.0), axis=0, keepdims=True) for k in range(3)
    )
    key_row = d0 * 65536.0 + d1 * 256.0 + d2
    low_row = jnp.floor(d0 * (1.0 / high)) * (high * 65536.0)
    key_col = jnp.transpose(jnp.broadcast_to(key_row, (8, total)))[:, 0:1]

    late[:, :keep] = recv[:, shift:shift + keep]
    if rest:
        a, b = iota((TILE, TILE), 0), iota((TILE, TILE), 1)
        v = a % SUB
        for t in range(band // TILE):
            rows_t = slice(t * TILE, (t + 1) * TILE)
            found = jnp.zeros((TILE, rest), F32)
            for j in range(per):
                pick = (a // SUB == b // SUB) & (v < tail) & (v % per == j) & (b % SUB == tail + v // per)
                found += jnp.dot(
                    hot_of(pick), recv[rows_t, shift + j * rest:shift + (j + 1) * rest],
                    preferred_element_type=F32)
            late[rows_t, keep:] = found.astype(BF16)

    def part(p, lo, hi):
        return recv[lo:hi, p * width:(p + 1) * width] if p < full else late[lo:hi, :]

    for t in range(total // TILE):
        lanes = slice(t * TILE, (t + 1) * TILE)
        p, lo = t * TILE // band, t * TILE % band
        query = part(p, lo, lo + TILE)
        best = jnp.full((1, TILE), -1.0, F32)
        for q in range(parts):
            cosine = lax.dot_general(part(q, 0, band), query, NT, preferred_element_type=F32)
            keys = key_col[q * band:(q + 1) * band]
            usable = (keys >= low_row[:, lanes]) & (keys < key_row[:, lanes])
            best = jnp.maximum(best, jnp.max(jnp.where(usable, cosine, -1.0), axis=0, keepdims=True))
        for w in range(TILE // 128):
            back[lo // 128 + w, p:p + 1, :] = best[:, w * 128:(w + 1) * 128]

    def back_copy(i):
        g, b = peer(i, -1)
        return pltpu.make_async_remote_copy(
            src_ref=back.at[((g * blocks + b) * SUB) // 128], dst_ref=home.at[i],
            send_sem=bsend_sem, recv_sem=brecv_sem,
            device_id={"group": g, "blk": b}, device_id_type=MESH,
        )

    others(lambda i: back_copy(i).start())
    own_back = pltpu.make_async_copy(back.at[(me * SUB) // 128], home.at[n // 2], self_sem)
    own_back.start()
    own_back.wait()

    def all_back():
        g, b = peer(0, -1)
        most = home.at[pl.ds(0, n - 1)]
        return pltpu.make_async_remote_copy(
            src_ref=most, dst_ref=most, send_sem=bsend_sem, recv_sem=brecv_sem,
            device_id={"group": g, "blk": b}, device_id_type=MESH)

    all_back().wait_recv()

    found = jnp.zeros((128, rows), F32)
    for p in range(parts):
        found += lax.dot_general(
            home[:, p, :], jnp.where(rank // SUB == p, hot, 0.0), TN,
            precision=lax.Precision.HIGHEST, preferred_element_type=F32)
    off = lax.rem(me * SUB, 128)
    result = jnp.sum(jnp.where(lane == rank % SUB + off, found, 0.0), axis=0, keepdims=True)
    out_ref[...] = result.reshape(rows)
    all_rows().wait_send()
    all_back().wait_send()


def on_device(embeddings, cluster, global_index, send_counts):
    rows, width = embeddings.shape
    groups = lax.axis_size("group")
    blocks = lax.axis_size("blk")
    n = groups * blocks
    capacity = -(-(3 * rows // (2 * groups)) // blocks)
    full, tail = capacity // SUB, capacity % SUB
    for keep in (width // 2, 3 * width // 4, width):
        rest = width - keep
        if tail + (-(-tail // (keep // rest)) if rest else 0) < SUB:
            break
    high = (n * rows - 1) // 65536 + 1
    band = n * SUB
    lanes = full * width + keep
    anywhere = pl.BlockSpec(memory_space=pltpu.HBM)
    return pl.pallas_call(
        functools.partial(kernel, groups, blocks, full, tail, keep, high),
        out_shape=jax.ShapeDtypeStruct((rows,), F32),
        in_specs=[anywhere] * 4,
        out_specs=pl.BlockSpec(memory_space=pltpu.VMEM),
        scratch_shapes=[
            pltpu.VMEM((1, groups), jnp.int32),
            pltpu.VMEM((rows,), jnp.int32),
            pltpu.VMEM((rows,), jnp.int32),
            pltpu.VMEM((rows, width), F32),
            pltpu.VMEM((band, lanes), BF16),
            pltpu.VMEM((band, lanes), BF16),
            pltpu.VMEM((rows, width), BF16),
            pltpu.VMEM((band, width), BF16),
            pltpu.VMEM((band // 128, full + 1, 128), F32),
            pltpu.VMEM((n, full + 1, 128), F32),
            pltpu.SemaphoreType.DMA((4,)),
            pltpu.SemaphoreType.DMA,
            pltpu.SemaphoreType.DMA,
            pltpu.SemaphoreType.DMA,
            pltpu.SemaphoreType.DMA,
            pltpu.SemaphoreType.DMA,
        ],
        compiler_params=pltpu.CompilerParams(
            collective_id=0, has_side_effects=True, vmem_limit_bytes=63 * 1024 * 1024
        ),
    )(send_counts, cluster, global_index, embeddings)


def solution(mesh):
    placed = (
        P(("group", "blk"), None),
        P(("group", "blk")),
        P(("group", "blk")),
        P(("group", "blk"), None),
    )
    return jax.shard_map(
        on_device, mesh=mesh, in_specs=placed, out_specs=P(("group", "blk")), check_vma=False
    )
```

```python
import functools

import jax
import jax.numpy as jnp
from jax import lax
from jax.experimental import pallas as pl
from jax.experimental.pallas import tpu as pltpu
from jax.sharding import PartitionSpec as P

CLUSTERS = 64
SUB = 16
SPAN = 32
TILE = 256
MESH = pl.DeviceIdType.MESH
NT = (((1,), (1,)), ((), ()))
TN = (((0,), (0,)), ((), ()))
F32 = jnp.float32
BF16 = jnp.bfloat16


def iota(shape, dim):
    return lax.broadcasted_iota(jnp.int32, shape, dim)


def hot_of(mask):
    return mask.astype(F32).astype(BF16)


def kernel(groups, blocks, full, tail, keep, high, cnt_hbm, cl_hbm, gid_hbm, emb_hbm, out_ref,
           cnt_ref, cl_ref, gid_ref, emb_ref, packed, recv, unit, late, back, home,
           in_sem, send_sem, recv_sem, bsend_sem, brecv_sem, self_sem):
    rows, width = emb_ref.shape
    n = groups * blocks
    band = n * SUB
    parts = full + 1
    per_block = CLUSTERS // blocks
    lows = blocks // 2
    rest = width - keep
    per = keep // rest if rest else 1
    shift = full * width
    my_g = lax.axis_index("group")
    my_b = lax.axis_index("blk")
    my_hi, my_lo = my_b // lows, lax.rem(my_b, lows)

    def peer(i, way):
        hi = lax.rem(my_hi + 1 - i // (n // 2), 2)
        j = lax.rem(i, n // 2)
        dl, dg = j // groups, lax.rem(j, groups)
        if way < 0:
            dl, dg = lows - dl, groups - dg
        lo = lax.rem(my_lo + dl, lows)
        g = lax.rem(my_g + dg, groups)
        return g, hi * lows + lo

    def others(act, lo=0, hi=None):
        hi = n if hi is None else hi

        def body(i, c):
            act(i)
            return c

        if lo < n // 2:
            lax.fori_loop(lo, min(hi, n // 2), body, 0)
        if hi > n // 2 + 1:
            lax.fori_loop(max(lo, n // 2 + 1), hi, body, 0)

    loads = [
        pltpu.make_async_copy(a, b, in_sem.at[k])
        for k, (a, b) in enumerate(
            ((cnt_hbm, cnt_ref), (cl_hbm, cl_ref), (gid_hbm, gid_ref), (emb_hbm, emb_ref)))
    ]
    for load in loads:
        load.start()

    barrier = pltpu.get_barrier_semaphore()

    def greet(i):
        g, b = peer(i, 1)
        pl.semaphore_signal(barrier, inc=1, device_id={"group": g, "blk": b}, device_id_type=MESH)

    others(greet)

    for load in loads[:3]:
        load.wait()
    pos = iota((1, rows), 1)
    owner = jnp.zeros((1, rows), jnp.int32)
    end = jnp.zeros((1, 1), jnp.int32)
    for g in range(groups - 1):
        end = end + cnt_ref[0:1, g:g + 1]
        owner += (pos >= end).astype(jnp.int32)
    cl = cl_ref[...].reshape(1, rows)
    gid = gid_ref[...].reshape(1, rows)
    to_b = cl // per_block
    to_hi, to_lo = to_b // lows, to_b % lows
    step = (
        jnp.where(to_hi == my_hi, n // 2, 0)
        + ((to_lo + lows - my_lo) % lows) * groups
        + (owner + groups - my_g) % groups
    )
    hot = (iota((n, rows), 0) == step).astype(F32)
    hot_b = hot.astype(BF16)
    upper = hot_of(iota((rows, rows), 0) < iota((rows, rows), 1))
    before = jnp.dot(hot_b, upper, preferred_element_type=F32)
    rank = jnp.sum(hot * before, axis=0, keepdims=True).astype(jnp.int32)
    u = rank - full * SUB
    first = step * SUB

    digits = (
        (cl % per_block + 1) * high + gid // 65536,
        (gid // 256) % 256,
        gid % 256,
    )
    lane = iota((128, rows), 0)
    spots = jnp.zeros((128, rows), F32)
    for k, d in enumerate(digits):
        spots = jnp.where(lane == rank + k * SPAN, d.astype(F32), spots)
    meta = lax.dot_general(hot_b, spots.astype(BF16), NT, preferred_element_type=F32).astype(BF16)

    slots = [jnp.where(rank // SUB == p, first + rank % SUB, -1) for p in range(full)]
    slots.append(jnp.where(u >= 0, first + u, -1))
    if rest:
        slots += [jnp.where((u >= 0) & (u % per == j), first + tail + u // per, -1) for j in range(per)]

    loads[3].wait()
    x = emb_ref[...]
    squares = jnp.sum(x * x, axis=1, keepdims=True)
    unit[...] = (x * lax.rsqrt(squares + 1e-06)).astype(BF16)

    half = band // 2
    place = my_g * lows + my_lo

    def mine(far):
        return pl.ds(pl.multiple_of(far * half + place * SUB, SUB), SUB)

    def out_copy(i):
        g, b = peer(i, 1)
        return pltpu.make_async_remote_copy(
            src_ref=packed.at[pl.ds(pl.multiple_of(i * SUB, SUB), SUB)],
            dst_ref=recv.at[mine(i // (n // 2))],
            send_sem=send_sem, recv_sem=recv_sem.at[i // (n // 2)],
            device_id={"group": g, "blk": b}, device_id_type=MESH,
        )

    for t in range(band // TILE):
        rows_t = slice(t * TILE, (t + 1) * TILE)
        at_row = iota((TILE, rows), 0) + t * TILE
        for p in range(full):
            packed[rows_t, p * width:(p + 1) * width] = jnp.dot(
                hot_of(at_row == slots[p]), unit[...], preferred_element_type=F32).astype(BF16)
        last = jnp.dot(hot_of(at_row == slots[full]), unit[:, :keep], preferred_element_type=F32)
        if rest:
            extra = [
                jnp.dot(hot_of(at_row == slots[full + 1 + j]), unit[:, keep:], preferred_element_type=F32)
                for j in range(per)
            ]
            last += jnp.concatenate(extra, axis=1)
        where = hot_of(iota((TILE, n), 0) + t * TILE == iota((TILE, n), 1) * SUB + SUB - 1)
        info = jnp.dot(where, meta, preferred_element_type=F32)
        packed[rows_t, shift:shift + 128] = (last[:, :128] + info).astype(BF16)
        packed[rows_t, shift + 128:shift + keep] = last[:, 128:].astype(BF16)
        if t == 0:
            pl.semaphore_wait(barrier, n - 1)
        others(lambda i: out_copy(i).start(), t * TILE // SUB, (t + 1) * TILE // SUB)

    own = pltpu.make_async_copy(packed.at[pl.ds(band // 2, SUB)], recv.at[mine(1)], self_sem)
    own.start()
    own.wait()

    def many(count, k):
        g, b = peer(0, 1)
        most = pl.ds(0, count * SUB)
        return pltpu.make_async_remote_copy(
            src_ref=packed.at[most], dst_ref=recv.at[most], send_sem=send_sem, recv_sem=recv_sem.at[k],
            device_id={"group": g, "blk": b}, device_id_type=MESH)

    def ready(h):
        base = h * half
        m = n // 2
        total = parts * half
        take = hot_of(iota((m, half), 1) == iota((m, half), 0) * SUB + SUB - 1)
        info = jnp.dot(take, recv[base:base + half, shift:shift + 128], preferred_element_type=F32)
        which = iota((m, 128), 1) // SPAN
        info = jnp.concatenate([jnp.where(which == k, info, 0.0) for k in range(3)], axis=0).astype(BF16)
        at = iota((128, total), 1)
        spread = hot_of(iota((128, total), 0) % SPAN == at // half * SUB + at % SUB)
        wide = jnp.dot(info, spread, preferred_element_type=F32)
        source = (iota((m, total), 1) % half) // SUB == iota((m, total), 0)
        d0, d1, d2 = (
            jnp.sum(jnp.where(source, wide[k * m:(k + 1) * m], 0.0), axis=0, keepdims=True)
            for k in range(3)
        )
        key_row = d0 * 65536.0 + d1 * 256.0 + d2
        low_row = jnp.floor(d0 * (1.0 / high)) * (high * 65536.0)
        key_col = jnp.transpose(jnp.broadcast_to(key_row, (8, total)))[:, 0:1]
        late[base:base + half, :keep] = recv[base:base + half, shift:shift + keep]
        if rest:
            a, b = iota((TILE, TILE), 0), iota((TILE, TILE), 1)
            v = a % SUB
            for t in range(half // TILE):
                rows_t = slice(base + t * TILE, base + (t + 1) * TILE)
                found = jnp.zeros((TILE, rest), F32)
                for j in range(per):
                    pick = (a // SUB == b // SUB) & (v < tail) & (v % per == j) & (b % SUB == tail + v // per)
                    found += jnp.dot(
                        hot_of(pick), recv[rows_t, shift + j * rest:shift + (j + 1) * rest],
                        preferred_element_type=F32)
                late[rows_t, keep:] = found.astype(BF16)
        return key_row, low_row, key_col

    def part(p, lo, hi):
        return recv[lo:hi, p * width:(p + 1) * width] if p < full else late[lo:hi, :]

    known = {}
    tiles = half // TILE
    bests = {}

    def meet(hq, hk):
        key_row, low_row = known[hq][0], known[hq][1]
        key_col = known[hk][2]
        for p in range(parts):
            for t in range(tiles):
                query = part(p, hq * half + t * TILE, hq * half + (t + 1) * TILE)
                lanes = slice(p * half + t * TILE, p * half + (t + 1) * TILE)
                best = bests.get((hq, p, t), jnp.full((1, TILE), -1.0, F32))
                for q in range(parts):
                    cosine = lax.dot_general(
                        part(q, hk * half, (hk + 1) * half), query, NT, preferred_element_type=F32)
                    keys = key_col[q * half:(q + 1) * half]
                    usable = (keys >= low_row[:, lanes]) & (keys < key_row[:, lanes])
                    best = jnp.maximum(best, jnp.max(jnp.where(usable, cosine, -1.0), axis=0, keepdims=True))
                bests[(hq, p, t)] = best

    many(n // 2 - 1, 1).wait_recv()
    known[1] = ready(1)
    meet(1, 1)
    many(n // 2, 0).wait_recv()
    known[0] = ready(0)
    meet(0, 0)
    meet(0, 1)
    meet(1, 0)
    for (h, p, t), best in bests.items():
        for w in range(TILE // 128):
            back[(h * half + t * TILE) // 128 + w, p:p + 1, :] = best[:, w * 128:(w + 1) * 128]

    def back_copy(i):
        g, b = peer(i, -1)
        return pltpu.make_async_remote_copy(
            src_ref=back.at[(i // (n // 2) * half + (g * lows + lax.rem(b, lows)) * SUB) // 128], dst_ref=home.at[i],
            send_sem=bsend_sem, recv_sem=brecv_sem,
            device_id={"group": g, "blk": b}, device_id_type=MESH,
        )

    others(lambda i: back_copy(i).start())
    own_back = pltpu.make_async_copy(back.at[(half + place * SUB) // 128], home.at[n // 2], self_sem)
    own_back.start()
    own_back.wait()

    def all_back():
        g, b = peer(0, -1)
        most = home.at[pl.ds(0, n - 1)]
        return pltpu.make_async_remote_copy(
            src_ref=most, dst_ref=most, send_sem=bsend_sem, recv_sem=brecv_sem,
            device_id={"group": g, "blk": b}, device_id_type=MESH)

    all_back().wait_recv()

    found = jnp.zeros((128, rows), F32)
    for p in range(parts):
        found += lax.dot_general(
            home[:, p, :], jnp.where(rank // SUB == p, hot, 0.0), TN,
            precision=lax.Precision.HIGHEST, preferred_element_type=F32)
    off = lax.rem(place * SUB, 128)
    result = jnp.sum(jnp.where(lane == rank % SUB + off, found, 0.0), axis=0, keepdims=True)
    out_ref[...] = result.reshape(rows)
    many(n - 1, 0).wait_send()
    all_back().wait_send()


def on_device(embeddings, cluster, global_index, send_counts):
    rows, width = embeddings.shape
    groups = lax.axis_size("group")
    blocks = lax.axis_size("blk")
    n = groups * blocks
    capacity = -(-(3 * rows // (2 * groups)) // blocks)
    full, tail = capacity // SUB, capacity % SUB
    for keep in (width // 2, 3 * width // 4, width):
        rest = width - keep
        if tail + (-(-tail // (keep // rest)) if rest else 0) < SUB:
            break
    high = (n * rows - 1) // 65536 + 1
    band = n * SUB
    lanes = full * width + keep
    anywhere = pl.BlockSpec(memory_space=pltpu.HBM)
    return pl.pallas_call(
        functools.partial(kernel, groups, blocks, full, tail, keep, high),
        out_shape=jax.ShapeDtypeStruct((rows,), F32),
        in_specs=[anywhere] * 4,
        out_specs=pl.BlockSpec(memory_space=pltpu.VMEM),
        scratch_shapes=[
            pltpu.VMEM((1, groups), jnp.int32),
            pltpu.VMEM((rows,), jnp.int32),
            pltpu.VMEM((rows,), jnp.int32),
            pltpu.VMEM((rows, width), F32),
            pltpu.VMEM((band, lanes), BF16),
            pltpu.VMEM((band, lanes), BF16),
            pltpu.VMEM((rows, width), BF16),
            pltpu.VMEM((band, width), BF16),
            pltpu.VMEM((band // 128, full + 1, 128), F32),
            pltpu.VMEM((n, full + 1, 128), F32),
            pltpu.SemaphoreType.DMA((4,)),
            pltpu.SemaphoreType.DMA,
            pltpu.SemaphoreType.DMA((2,)),
            pltpu.SemaphoreType.DMA,
            pltpu.SemaphoreType.DMA,
            pltpu.SemaphoreType.DMA,
        ],
        compiler_params=pltpu.CompilerParams(
            collective_id=0, has_side_effects=True, vmem_limit_bytes=63 * 1024 * 1024
        ),
    )(send_counts, cluster, global_index, embeddings)


def solution(mesh):
    placed = (
        P(("group", "blk"), None),
        P(("group", "blk")),
        P(("group", "blk")),
        P(("group", "blk"), None),
    )
    return jax.shard_map(
        on_device, mesh=mesh, in_specs=placed, out_specs=P(("group", "blk")), check_vma=False
    )
```

```python
import functools

import jax
import jax.numpy as jnp
from jax import lax
from jax.experimental import pallas as pl
from jax.experimental.pallas import tpu as pltpu
from jax.sharding import PartitionSpec as P

CLUSTERS = 64
SUB = 16
SPAN = 32
TILE = 256
MESH = pl.DeviceIdType.MESH
NT = (((1,), (1,)), ((), ()))
TN = (((0,), (0,)), ((), ()))
F32 = jnp.float32
BF16 = jnp.bfloat16


def iota(shape, dim):
    return lax.broadcasted_iota(jnp.int32, shape, dim)


def hot_of(mask):
    return mask.astype(F32).astype(BF16)


def kernel(groups, blocks, full, tail, keep, high, cnt_hbm, cl_hbm, gid_hbm, emb_hbm, out_ref,
           cnt_ref, cl_ref, gid_ref, emb_ref, packed, recv, unit, late, back, home,
           in_sem, send_sem, recv_sem, bsend_sem, brecv_sem, self_sem):
    rows, width = emb_ref.shape
    n = groups * blocks
    band = n * SUB
    parts = full + 1
    per_block = CLUSTERS // blocks
    lows = blocks // 2
    rest = width - keep
    per = keep // rest if rest else 1
    shift = full * width
    my_g = lax.axis_index("group")
    my_b = lax.axis_index("blk")
    my_hi, my_lo = my_b // lows, lax.rem(my_b, lows)

    def peer(i, way):
        hi = lax.rem(my_hi + 1 - i // (n // 2), 2)
        j = lax.rem(i, n // 2)
        dl, dg = j // groups, lax.rem(j, groups)
        if way < 0:
            dl, dg = lows - dl, groups - dg
        lo = lax.rem(my_lo + dl, lows)
        g = lax.rem(my_g + dg, groups)
        return g, hi * lows + lo

    def others(act, lo=0, hi=None):
        hi = n if hi is None else hi

        def body(i, c):
            act(i)
            return c

        if lo < n // 2:
            lax.fori_loop(lo, min(hi, n // 2), body, 0)
        if hi > n // 2 + 1:
            lax.fori_loop(max(lo, n // 2 + 1), hi, body, 0)

    loads = [
        pltpu.make_async_copy(a, b, in_sem.at[k])
        for k, (a, b) in enumerate(
            ((cnt_hbm, cnt_ref), (cl_hbm, cl_ref), (gid_hbm, gid_ref), (emb_hbm, emb_ref)))
    ]
    for load in loads:
        load.start()

    barrier = pltpu.get_barrier_semaphore()

    def greet(i):
        g, b = peer(i, 1)
        pl.semaphore_signal(barrier, inc=1, device_id={"group": g, "blk": b}, device_id_type=MESH)

    others(greet)

    for load in loads[:3]:
        load.wait()
    pos = iota((1, rows), 1)
    owner = jnp.zeros((1, rows), jnp.int32)
    end = jnp.zeros((1, 1), jnp.int32)
    for g in range(groups - 1):
        end = end + cnt_ref[0:1, g:g + 1]
        owner += (pos >= end).astype(jnp.int32)
    cl = cl_ref[...].reshape(1, rows)
    gid = gid_ref[...].reshape(1, rows)
    to_b = cl // per_block
    to_hi, to_lo = to_b // lows, to_b % lows
    step = (
        jnp.where(to_hi == my_hi, n // 2, 0)
        + ((to_lo + lows - my_lo) % lows) * groups
        + (owner + groups - my_g) % groups
    )
    hot = (iota((n, rows), 0) == step).astype(F32)
    hot_b = hot.astype(BF16)
    upper = hot_of(iota((rows, rows), 0) < iota((rows, rows), 1))
    before = jnp.dot(hot_b, upper, preferred_element_type=F32)
    rank = jnp.sum(hot * before, axis=0, keepdims=True).astype(jnp.int32)
    u = rank - full * SUB
    first = step * SUB

    digits = (
        (cl % per_block + 1) * high + gid // 65536,
        (gid // 256) % 256,
        gid % 256,
    )
    lane = iota((128, rows), 0)
    spots = jnp.zeros((128, rows), F32)
    for k, d in enumerate(digits):
        spots = jnp.where(lane == rank + k * SPAN, d.astype(F32), spots)
    meta = lax.dot_general(hot_b, spots.astype(BF16), NT, preferred_element_type=F32).astype(BF16)

    slots = [jnp.where(rank // SUB == p, first + rank % SUB, -1) for p in range(full)]
    slots.append(jnp.where(u >= 0, first + u, -1))
    if rest:
        slots += [jnp.where((u >= 0) & (u % per == j), first + tail + u // per, -1) for j in range(per)]

    loads[3].wait()
    x = emb_ref[...]
    squares = jnp.sum(x * x, axis=1, keepdims=True)
    unit[...] = (x * lax.rsqrt(squares + 1e-06)).astype(BF16)

    half = band // 2
    place = my_g * lows + my_lo

    def mine(far):
        return pl.ds(pl.multiple_of(far * half + place * SUB, SUB), SUB)

    def out_copy(i):
        g, b = peer(i, 1)
        return pltpu.make_async_remote_copy(
            src_ref=packed.at[pl.ds(pl.multiple_of(i * SUB, SUB), SUB)],
            dst_ref=recv.at[mine(i // (n // 2))],
            send_sem=send_sem, recv_sem=recv_sem.at[i // (n // 2)],
            device_id={"group": g, "blk": b}, device_id_type=MESH,
        )

    for t in range(band // TILE):
        rows_t = slice(t * TILE, (t + 1) * TILE)
        at_row = iota((TILE, rows), 0) + t * TILE
        for p in range(full):
            packed[rows_t, p * width:(p + 1) * width] = jnp.dot(
                hot_of(at_row == slots[p]), unit[...], preferred_element_type=F32).astype(BF16)
        last = jnp.dot(hot_of(at_row == slots[full]), unit[:, :keep], preferred_element_type=F32)
        if rest:
            extra = [
                jnp.dot(hot_of(at_row == slots[full + 1 + j]), unit[:, keep:], preferred_element_type=F32)
                for j in range(per)
            ]
            last += jnp.concatenate(extra, axis=1)
        where = hot_of(iota((TILE, n), 0) + t * TILE == iota((TILE, n), 1) * SUB + SUB - 1)
        info = jnp.dot(where, meta, preferred_element_type=F32)
        packed[rows_t, shift:shift + 128] = (last[:, :128] + info).astype(BF16)
        packed[rows_t, shift + 128:shift + keep] = last[:, 128:].astype(BF16)
        if t == 0:
            pl.semaphore_wait(barrier, n - 1)
        others(lambda i: out_copy(i).start(), t * TILE // SUB, (t + 1) * TILE // SUB)

    own = pltpu.make_async_copy(packed.at[pl.ds(band // 2, SUB)], recv.at[mine(1)], self_sem)
    own.start()
    own.wait()

    def many(count, k):
        g, b = peer(0, 1)
        most = pl.ds(0, count * SUB)
        return pltpu.make_async_remote_copy(
            src_ref=packed.at[most], dst_ref=recv.at[most], send_sem=send_sem, recv_sem=recv_sem.at[k],
            device_id={"group": g, "blk": b}, device_id_type=MESH)

    def ready(h):
        base = h * half
        m = n // 2
        total = parts * half
        take = hot_of(iota((m, half), 1) == iota((m, half), 0) * SUB + SUB - 1)
        info = jnp.dot(take, recv[base:base + half, shift:shift + 128], preferred_element_type=F32)
        which = iota((m, 128), 1) // SPAN
        info = jnp.concatenate([jnp.where(which == k, info, 0.0) for k in range(3)], axis=0).astype(BF16)
        at = iota((128, total), 1)
        spread = hot_of(iota((128, total), 0) % SPAN == at // half * SUB + at % SUB)
        wide = jnp.dot(info, spread, preferred_element_type=F32)
        source = (iota((m, total), 1) % half) // SUB == iota((m, total), 0)
        d0, d1, d2 = (
            jnp.sum(jnp.where(source, wide[k * m:(k + 1) * m], 0.0), axis=0, keepdims=True)
            for k in range(3)
        )
        key_row = d0 * 65536.0 + d1 * 256.0 + d2
        low_row = jnp.floor(d0 * (1.0 / high)) * (high * 65536.0)
        key_col = jnp.transpose(jnp.broadcast_to(key_row, (8, total)))[:, 0:1]
        late[base:base + half, :keep] = recv[base:base + half, shift:shift + keep]
        if rest:
            a, b = iota((TILE, TILE), 0), iota((TILE, TILE), 1)
            v = a % SUB
            for t in range(half // TILE):
                rows_t = slice(base + t * TILE, base + (t + 1) * TILE)
                found = jnp.zeros((TILE, rest), F32)
                for j in range(per):
                    pick = (a // SUB == b // SUB) & (v < tail) & (v % per == j) & (b % SUB == tail + v // per)
                    found += jnp.dot(
                        hot_of(pick), recv[rows_t, shift + j * rest:shift + (j + 1) * rest],
                        preferred_element_type=F32)
                late[rows_t, keep:] = found.astype(BF16)
        return key_row, low_row, key_col

    def part(p, lo, hi):
        return recv[lo:hi, p * width:(p + 1) * width] if p < full else late[lo:hi, :]

    known = {}
    tiles = half // TILE
    bests = {}

    def meet(hq, hk):
        key_row, low_row = known[hq][0], known[hq][1]
        key_col = known[hk][2]
        for p in range(parts):
            for t in range(tiles):
                query = part(p, hq * half + t * TILE, hq * half + (t + 1) * TILE)
                lanes = slice(p * half + t * TILE, p * half + (t + 1) * TILE)
                best = bests.get((hq, p, t), jnp.full((1, TILE), -1.0, F32))
                for q in range(parts):
                    cosine = lax.dot_general(
                        part(q, hk * half, (hk + 1) * half), query, NT, preferred_element_type=F32)
                    keys = key_col[q * half:(q + 1) * half]
                    usable = (keys >= low_row[:, lanes]) & (keys < key_row[:, lanes])
                    best = jnp.maximum(best, jnp.max(jnp.where(usable, cosine, -1.0), axis=0, keepdims=True))
                bests[(hq, p, t)] = best

    def keep_best(half_no):
        for (h, p, t), best in bests.items():
            if h == half_no:
                for w in range(TILE // 128):
                    back[(h * half + t * TILE) // 128 + w, p:p + 1, :] = best[:, w * 128:(w + 1) * 128]

    def back_copy(i):
        g, b = peer(i, -1)
        return pltpu.make_async_remote_copy(
            src_ref=back.at[(i // (n // 2) * half + (g * lows + lax.rem(b, lows)) * SUB) // 128], dst_ref=home.at[i],
            send_sem=bsend_sem, recv_sem=brecv_sem,
            device_id={"group": g, "blk": b}, device_id_type=MESH,
        )

    many(n // 2 - 1, 1).wait_recv()
    known[1] = ready(1)
    meet(1, 1)
    many(n // 2, 0).wait_recv()
    known[0] = ready(0)
    meet(0, 0)
    meet(0, 1)
    keep_best(0)
    others(lambda i: back_copy(i).start(), 0, n // 2)
    meet(1, 0)
    keep_best(1)
    others(lambda i: back_copy(i).start(), n // 2, n)
    own_back = pltpu.make_async_copy(back.at[(half + place * SUB) // 128], home.at[n // 2], self_sem)
    own_back.start()
    own_back.wait()

    def all_back():
        g, b = peer(0, -1)
        most = home.at[pl.ds(0, n - 1)]
        return pltpu.make_async_remote_copy(
            src_ref=most, dst_ref=most, send_sem=bsend_sem, recv_sem=brecv_sem,
            device_id={"group": g, "blk": b}, device_id_type=MESH)

    all_back().wait_recv()

    found = jnp.zeros((128, rows), F32)
    for p in range(parts):
        found += lax.dot_general(
            home[:, p, :], jnp.where(rank // SUB == p, hot, 0.0), TN,
            precision=lax.Precision.HIGHEST, preferred_element_type=F32)
    off = lax.rem(place * SUB, 128)
    result = jnp.sum(jnp.where(lane == rank % SUB + off, found, 0.0), axis=0, keepdims=True)
    out_ref[...] = result.reshape(rows)
    many(n - 1, 0).wait_send()
    all_back().wait_send()


def on_device(embeddings, cluster, global_index, send_counts):
    rows, width = embeddings.shape
    groups = lax.axis_size("group")
    blocks = lax.axis_size("blk")
    n = groups * blocks
    capacity = -(-(3 * rows // (2 * groups)) // blocks)
    full, tail = capacity // SUB, capacity % SUB
    for keep in (width // 2, 3 * width // 4, width):
        rest = width - keep
        if tail + (-(-tail // (keep // rest)) if rest else 0) < SUB:
            break
    high = (n * rows - 1) // 65536 + 1
    band = n * SUB
    lanes = full * width + keep
    anywhere = pl.BlockSpec(memory_space=pltpu.HBM)
    return pl.pallas_call(
        functools.partial(kernel, groups, blocks, full, tail, keep, high),
        out_shape=jax.ShapeDtypeStruct((rows,), F32),
        in_specs=[anywhere] * 4,
        out_specs=pl.BlockSpec(memory_space=pltpu.VMEM),
        scratch_shapes=[
            pltpu.VMEM((1, groups), jnp.int32),
            pltpu.VMEM((rows,), jnp.int32),
            pltpu.VMEM((rows,), jnp.int32),
            pltpu.VMEM((rows, width), F32),
            pltpu.VMEM((band, lanes), BF16),
            pltpu.VMEM((band, lanes), BF16),
            pltpu.VMEM((rows, width), BF16),
            pltpu.VMEM((band, width), BF16),
            pltpu.VMEM((band // 128, full + 1, 128), F32),
            pltpu.VMEM((n, full + 1, 128), F32),
            pltpu.SemaphoreType.DMA((4,)),
            pltpu.SemaphoreType.DMA,
            pltpu.SemaphoreType.DMA((2,)),
            pltpu.SemaphoreType.DMA,
            pltpu.SemaphoreType.DMA,
            pltpu.SemaphoreType.DMA,
        ],
        compiler_params=pltpu.CompilerParams(
            collective_id=0, has_side_effects=True, vmem_limit_bytes=63 * 1024 * 1024
        ),
    )(send_counts, cluster, global_index, embeddings)


def solution(mesh):
    placed = (
        P(("group", "blk"), None),
        P(("group", "blk")),
        P(("group", "blk")),
        P(("group", "blk"), None),
    )
    return jax.shard_map(
        on_device, mesh=mesh, in_specs=placed, out_specs=P(("group", "blk")), check_vma=False
    )
```
